32 devices in a mesh: dp: 4 (over x, core), expert: 8 (over z, y).
Axes of the slice: x: 2, y: 2, z: 4, core: 2. Of those that a mesh axis runs over, the one named last changes fastest.
Arguments:
- tokens: bfloat16 [1024, 3584], P('expert', 'dp'), may hold values from -6 to 6
- routes: int32 [1024, 4], P('expert'), may hold values from 0 to 7, all different within a row; in each aligned block of 128 rows (0 to 127, 128 to 255, ...) at most 96 rows name the same one
- gates: float32 [1024, 4], P('expert'), may hold values from 0.1 to 1
- w_gate: bfloat16 [8, 3584, 1024], P('expert', 'dp'), may hold values from -0.09375 to 0.09375
- w_up: bfloat16 [8, 3584, 1024], P('expert', 'dp'), may hold values from -0.09375 to 0.09375
- w_down: bfloat16 [8, 1024, 3584], P('expert', None, 'dp'), may hold values from -0.1875 to 0.1875
- cotangent: bfloat16 [1024, 3584], P('expert', 'dp'), may hold values from -1.5 to 1.5
Outputs:
- mixed: bfloat16 [1024, 3584], P('expert', 'dp')
- token_grad: bfloat16 [1024, 3584], P('expert', 'dp')
- gate_grad: float32 [1024, 4], P('expert')
- w_gate_grad: bfloat16 [8, 3584, 1024], P('expert', 'dp')
- w_up_grad: bfloat16 [8, 3584, 1024], P('expert', 'dp')
- w_down_grad: bfloat16 [8, 1024, 3584], P('expert', None, 'dp')
The draws below stay inside these ranges and needn't reach their ends.
Inputs may be any that keep to these rules, and one draw needn't show every extreme that they name: `routes`: each row names 4 different experts. Within the 128 rows of one index of the expert axis (aligned blocks of rows), no expert is named more than 96 times, and in every draw some expert is named exactly 96 times in some block.
All inputs are finite; a program needn't handle non-finite values.
Results may differ from the reference program's by a relative error of at most 0.028.
Values may be sent and summed in bfloat16 or wider, within the bound.
A program may use at most 128 MiB of HBM per device.

```python
import math
import jax
import jax.numpy as jnp
import numpy as np
from jax import lax

D = 3584
HIDDEN_SIZE = 1024
TOK_DEV = 128
TOPK = 4
EXPERTS = 8
TOKENS = 1024
CAP = 96
N_DP = 4
N_EXPERT = 8


def block_levels(stream_key, extent, split, low, high):
    def one(dim, shards_of):
        steps = jax.random.uniform(jax.random.fold_in(jax.random.fold_in(stream_key, 6), dim), (shards_of,), jnp.float32, low / len(split), high / len(split))
        return jnp.repeat(jnp.exp(steps), extent[dim] // shards_of).reshape((-1,) + (1,) * (len(extent) - dim - 1))

    gain = one(*split[0])
    for cut in split[1:]:
        gain = gain * one(*cut)
    return gain


def shared_out(key, own, number, rows, number_of, top, most, lean):
    sequence = jax.random.permutation(key, number_of)
    packed, usual = portions_of(number_of, rows * top, most, lean, True), portions_of(number_of, rows * top, most, lean, False)
    places = jnp.arange(number_of)

    def named(lengths, offset_by):
        used = int((lengths > 0).sum())
        fixed = max(1, used // 4)
        shifted = fixed + (places - fixed + offset_by * (used - fixed)) % max(1, number_of - fixed)
        return jnp.zeros((number_of,), jnp.int32).at[sequence[jnp.where(places < fixed, places, shifted)]].set(jnp.asarray(lengths, jnp.int32))

    lengths = jnp.where(number % 4 == 0, named(packed, number // 4), named(usual, number - number // 4 - 1))
    mixed = jax.random.permutation(jax.random.fold_in(own, 3), number_of)
    donor, sink = mixed[0:number_of // 2 * 2:2], mixed[1:number_of // 2 * 2:2]
    slack = jnp.minimum(lengths[donor] - 1, most - lengths[sink]) // 2
    slack = jnp.where((donor == sequence[0]) | (sink == sequence[0]) | (lengths[sink] == 0), 0, jnp.maximum(slack, 0))
    shifted = jax.random.randint(jax.random.fold_in(own, 4), (number_of // 2,), 0, 1 << 20) % (slack + 1)
    lengths = lengths.at[donor].add(-shifted).at[sink].add(shifted)
    items = jnp.searchsorted(jnp.cumsum(lengths), jnp.arange(rows * top), side="right").astype(jnp.int32)
    listing = items.reshape(top, rows).T
    listing = listing[jax.random.permutation(jax.random.fold_in(own, 1), rows)]
    offset_by = jax.random.randint(jax.random.fold_in(own, 2), (rows, 1), 0, top)
    return jnp.take_along_axis(listing, (jnp.arange(top)[None, :] + offset_by) % top, axis=1)


def portions_of(number_of, total, most, skew, full):
    portions = [(1 << 20) // math.isqrt(standing ** skew) + 1 for standing in range(1, number_of + 1)]
    largest = most if full else min(most, max(-(-total // number_of), total * portions[0] // sum(portions)))
    least = 1 if total - largest >= number_of - 1 else 0
    holding, surplus = [largest] + [least] * (number_of - 1), total - largest - least * (number_of - 1)
    while surplus > 0:
        free = [i for i in range(1, number_of) if holding[i] < largest] or [i for i in range(1, number_of) if holding[i] < most]
        whole, budget = sum([portions[i] for i in free]), surplus
        for i in free:
            addition = min(most - holding[i], max(1, budget * portions[i] // whole), surplus)
            holding[i] = holding[i] + addition
            surplus = surplus - addition
    return np.array(holding)


def bell_draw(rng, dims, width, limit, shards=(), kind=jnp.bfloat16):
    drawn = width * jax.random.normal(rng, dims, jnp.float32)
    if shards:
        drawn = drawn * block_levels(rng, dims, shards, -0.22, 0.18)
    return jnp.clip(drawn, -limit, limit).astype(kind)


def setup_inputs(seed: int = 0) -> dict:
    seeds = jax.random.split(jax.random.key(seed), 8)
    tokens = bell_draw(seeds[0], (TOKENS, D), 1.0, 6.0, ((0, 8), (1, 4)))
    routes_keys = jax.random.split(jax.random.fold_in(seeds[1], 1), TOKENS // TOK_DEV)
    routes_turns = jax.random.permutation(jax.random.fold_in(seeds[1], 3), TOKENS // TOK_DEV)
    routes = jax.vmap(lambda own, number: shared_out(jax.random.fold_in(seeds[1], 2), own, number, TOK_DEV, EXPERTS, TOPK, CAP, 2))(routes_keys, routes_turns).reshape((TOKENS, TOPK))
    gates = jnp.clip(jnp.exp(math.log(1.0) - 2.3025851 * jax.random.uniform(seeds[2], (TOKENS, TOPK), jnp.float32) ** block_levels(seeds[2], (TOKENS, TOPK), ((0, 8),), -0.2, 0.2)), 0.1, 1.0)
    w_gate = bell_draw(seeds[3], (EXPERTS, D, HIDDEN_SIZE), D ** -0.5, 0.09375, ((0, 8), (1, 4)))
    w_up = bell_draw(seeds[4], (EXPERTS, D, HIDDEN_SIZE), D ** -0.5, 0.09375, ((0, 8), (1, 4)))
    w_down = bell_draw(seeds[5], (EXPERTS, HIDDEN_SIZE, D), HIDDEN_SIZE ** -0.5, 0.1875, ((0, 8), (2, 4)))
    cotangent = bell_draw(seeds[6], (TOKENS, D), 0.25, 1.5, ((0, 8), (1, 4)))
    return dict(tokens=tokens, routes=routes, gates=gates, w_gate=w_gate, w_up=w_up, w_down=w_down, cotangent=cotangent)


def block_sum(left, right):
    row_count = left.shape[0]
    block_width = left.shape[1] // N_DP
    left_blocks = left.reshape(row_count, N_DP, block_width).astype(jnp.float32)
    right_blocks = right.reshape(N_DP, block_width, right.shape[1]).astype(jnp.float32)
    partials = jnp.einsum('rbd,bdh->brh', left_blocks, right_blocks)
    rounded = lax.optimization_barrier(partials.astype(jnp.bfloat16))
    return lax.optimization_barrier(jnp.sum(rounded.astype(jnp.float32), axis=0))

def full_grad(left, right):
    return jnp.dot(left.T, right, preferred_element_type=jnp.float32).astype(jnp.bfloat16)

def slot_table(routes):
    flat_routes = routes.reshape(N_EXPERT, TOK_DEV * TOPK).astype(jnp.int32)
    labels = jnp.arange(EXPERTS, dtype=jnp.int32)
    onehot = (flat_routes[:, :, None] == labels[None, None, :]).astype(jnp.int32)
    earlier = jnp.cumsum(onehot, axis=1) - onehot
    rank_in = lax.optimization_barrier(jnp.sum(earlier * onehot, axis=2)).astype(jnp.int32)
    source = jnp.arange(N_EXPERT, dtype=jnp.int32)[:, None]
    position = flat_routes * (N_EXPERT * CAP) + source * CAP + rank_in
    pair_ids = jnp.arange(TOKENS * TOPK, dtype=jnp.int32)
    table = jnp.full((EXPERTS * N_EXPERT * CAP,), TOKENS * TOPK, jnp.int32)
    table = table.at[position.reshape(-1)].set(pair_ids)
    return table.reshape(EXPERTS, N_EXPERT * CAP)

def reference(tokens, routes, gates, w_gate, w_up, w_down, cotangent):
    none_row = TOKENS * TOPK
    table = slot_table(routes)
    token_pad = jnp.concatenate([tokens, jnp.zeros((1, D), jnp.bfloat16)], axis=0)
    scaled = (gates[:, :, None] * cotangent.astype(jnp.float32)[:, None, :]).astype(jnp.bfloat16)
    scaled_pad = jnp.concatenate([scaled.reshape(none_row, D), jnp.zeros((1, D), jnp.bfloat16)], axis=0)

    def expert_step(carry, inputs):
        outs_all, grads_all = carry
        slot_rows, gate_weight, up_weight, down_weight = inputs
        token_rows = jnp.where(slot_rows < none_row, slot_rows // TOPK, TOKENS).astype(jnp.int32)
        inputs_rows = token_pad[token_rows]
        cot_rows = scaled_pad[slot_rows]
        gate_pre = block_sum(inputs_rows, gate_weight)
        up_pre = block_sum(inputs_rows, up_weight)
        sigmoid_gate = jax.nn.sigmoid(gate_pre)
        active = gate_pre * sigmoid_gate
        hidden = (active * up_pre).astype(jnp.bfloat16)
        expert_out = jnp.dot(hidden, down_weight, preferred_element_type=jnp.float32).astype(jnp.bfloat16)
        hidden_grad = block_sum(cot_rows, down_weight.T)
        gate_pre_grad = (hidden_grad * up_pre * sigmoid_gate * (1.0 + gate_pre * (1.0 - sigmoid_gate))).astype(jnp.bfloat16)
        up_pre_grad = (hidden_grad * active).astype(jnp.bfloat16)
        pair_grad = (jnp.dot(gate_pre_grad, gate_weight.T, preferred_element_type=jnp.float32) + jnp.dot(up_pre_grad, up_weight.T, preferred_element_type=jnp.float32)).astype(jnp.bfloat16)
        gate_weight_grad = full_grad(inputs_rows, gate_pre_grad)
        up_weight_grad = full_grad(inputs_rows, up_pre_grad)
        down_weight_grad = full_grad(hidden, cot_rows)
        outs_all = outs_all.at[slot_rows].set(expert_out)
        grads_all = grads_all.at[slot_rows].set(pair_grad)
        return ((outs_all, grads_all), (gate_weight_grad, up_weight_grad, down_weight_grad))
    start = (jnp.zeros((none_row + 1, D), jnp.bfloat16), jnp.zeros((none_row + 1, D), jnp.bfloat16))
    (outs_all, grads_all), weight_grads = lax.scan(expert_step, start, (table, w_gate, w_up, w_down))
    expert_out = outs_all[:none_row].reshape(TOKENS, TOPK, D).astype(jnp.float32)
    mixed = lax.optimization_barrier(jnp.sum(gates[:, :, None] * expert_out, axis=1)).astype(jnp.bfloat16)
    gate_grad = lax.optimization_barrier(jnp.sum(expert_out * cotangent.astype(jnp.float32)[:, None, :], axis=2))
    token_grad = lax.optimization_barrier(jnp.sum(grads_all[:none_row].reshape(TOKENS, TOPK, D).astype(jnp.float32), axis=1)).astype(jnp.bfloat16)
    return (mixed, token_grad, gate_grad, weight_grads[0], weight_grads[1], weight_grads[2])
```

```python
import jax
import jax.numpy as jnp
from jax import lax
from jax.sharding import PartitionSpec as P

BF = jnp.bfloat16
F32 = jnp.float32


def dot(a, b):
    return jnp.dot(a, b, preferred_element_type=F32)


def dot_t(a, b):
    return lax.dot_general(a, b, (((0,), (0,)), ((), ())), preferred_element_type=F32)


def dot_nt(a, b):
    return lax.dot_general(a, b, (((1,), (1,)), ((), ())), preferred_element_type=F32)


def hop(v, bit):
    count = lax.axis_size("dp")
    return lax.ppermute(v, "dp", [(i, i ^ bit) for i in range(count)])


def reduce_rows(p):
    q = p.shape[0] // 4
    sent = jnp.concatenate([p[q:2 * q], p[3 * q:]], axis=0)
    got = hop(sent, 1)
    kept = p[:q].astype(F32) + got[:q].astype(F32)
    other = (p[2 * q:3 * q].astype(F32) + got[q:].astype(F32)).astype(BF)
    return kept + hop(other, 2).astype(F32)


def gather_rows(h):
    both = jnp.concatenate([h, hop(h, 2)], axis=0)
    far = hop(both, 1)
    q = h.shape[0]
    return jnp.concatenate([both[:q], far[:q], both[q:], far[q:]], axis=0)


def per_device(tokens, routes, gates, w_gate, w_up, w_down, cotangent):
    tok_rows, quarter = tokens.shape
    top_count = routes.shape[1]
    experts = lax.axis_size("expert")
    capacity = max(2, (3 * tok_rows * top_count + 2 * experts - 1) // (2 * experts))
    slots = experts * capacity
    q = slots // 4
    me = lax.axis_index("expert")
    d = lax.axis_index("dp")
    wg, wu, wd = w_gate[0], w_up[0], w_down[0]

    labels = jnp.arange(experts, dtype=jnp.int32)
    chosen = routes[:, :, None] == labels[None, None, :]
    table = jnp.sum(jnp.where(chosen, gates[:, :, None], 0.0), axis=1)
    weight = lax.all_to_all(table.T, "expert", split_axis=0, concat_axis=0, tiled=True)
    weight = weight.reshape(experts * tok_rows)
    x = lax.all_gather(tokens, "expert", axis=0, tiled=True)
    c = lax.all_gather(cotangent, "expert", axis=0, tiled=True)

    routed = weight > 0.0
    rank = jnp.cumsum(routed.astype(jnp.int32)) - 1
    rank = jnp.where(routed, rank, -1)
    place = jnp.arange(slots, dtype=jnp.int32)
    place = (place // q ^ d) * q + place % q
    hit = place[:, None] == rank[None, :]
    pick = hit.astype(BF)
    slot_gate = jnp.sum(jnp.where(hit, weight[None, :], 0.0), axis=1)

    xs = dot(pick, x).astype(BF)
    gate_pre = reduce_rows(dot(xs, wg).astype(BF))
    up_pre = reduce_rows(dot(xs, wu).astype(BF))
    cs = dot(pick, c).astype(BF)
    raw_grad = reduce_rows(dot_nt(cs, wd).astype(BF))

    own_gate = slot_gate[:q, None]
    sig = jax.nn.sigmoid(gate_pre)
    active = gate_pre * sig
    hidden32 = active * up_pre
    hidden = gather_rows(hidden32.astype(BF))
    gate_inner = jnp.sum(hidden32 * raw_grad, axis=1)
    hidden_grad = raw_grad * own_gate
    gpg = gather_rows((hidden_grad * up_pre * sig * (1.0 + gate_pre * (1.0 - sig))).astype(BF))
    upg = gather_rows((hidden_grad * active).astype(BF))

    out = (dot(hidden, wd) * slot_gate[:, None]).astype(BF)
    mixed = lax.psum_scatter(dot_t(pick, out).astype(BF), "expert", scatter_dimension=0, tiled=True)
    pair = (dot_nt(gpg, wg) + dot_nt(upg, wu)).astype(BF)
    token_grad = lax.psum_scatter(dot_t(pick, pair).astype(BF), "expert", scatter_dimension=0, tiled=True)

    inner = gather_rows(gate_inner[:, None])
    inner = jnp.sum(jnp.where(hit, inner, 0.0), axis=0).reshape(experts, tok_rows)
    inner = lax.all_to_all(inner, "expert", split_axis=0, concat_axis=0, tiled=True)
    gate_grad = jnp.sum(jnp.where(chosen, inner.T[:, None, :], 0.0), axis=2)

    w_down_grad = dot_t((hidden.astype(F32) * slot_gate[:, None]).astype(BF), cs).astype(BF)[None]
    w_gate_grad = dot_t(xs, gpg).astype(BF)[None]
    w_up_grad = dot_t(xs, upg).astype(BF)[None]
    return mixed, token_grad, gate_grad, w_gate_grad, w_up_grad, w_down_grad


def solution(mesh):
    placed = (
        P("expert", "dp"),
        P("expert", None),
        P("expert", None),
        P("expert", "dp", None),
        P("expert", "dp", None),
        P("expert", None, "dp"),
        P("expert", "dp"),
    )
    return jax.shard_map(
        per_device,
        mesh=mesh,
        in_specs=placed,
        out_specs=(
            P("expert", "dp"),
            P("expert", "dp"),
            P("expert", None),
            P("expert", "dp", None),
            P("expert", "dp", None),
            P("expert", None, "dp"),
        ),
        check_vma=False,
    )
```

```python
import functools

import jax
import jax.numpy as jnp
from jax import lax
from jax.experimental import pallas as pl
from jax.experimental.pallas import tpu as pltpu
from jax.sharding import PartitionSpec as P

BF = jnp.bfloat16
F32 = jnp.float32


def dot(a, b):
    return jnp.dot(a, b, preferred_element_type=F32)


def dot_t(a, b):
    return lax.dot_general(a, b, (((0,), (0,)), ((), ())), preferred_element_type=F32)


def dot_nt(a, b):
    return lax.dot_general(a, b, (((1,), (1,)), ((), ())), preferred_element_type=F32)


def hop(v, bit):
    count = lax.axis_size("dp")
    return lax.ppermute(v, "dp", [(i, i ^ bit) for i in range(count)])


def reduce_rows(p):
    q = p.shape[0] // 4
    sent = jnp.concatenate([p[q:2 * q], p[3 * q:]], axis=0)
    got = hop(sent, 1)
    kept = p[:q].astype(F32) + got[:q].astype(F32)
    other = (p[2 * q:3 * q].astype(F32) + got[q:].astype(F32)).astype(BF)
    return kept + hop(other, 2).astype(F32)


def gather_rows(h):
    both = jnp.concatenate([h, hop(h, 2)], axis=0)
    far = hop(both, 1)
    q = h.shape[0]
    return jnp.concatenate([both[:q], far[:q], both[q:], far[q:]], axis=0)


MESH = pl.DeviceIdType.MESH
VM = pl.BlockSpec(memory_space=pltpu.VMEM)


def greet(z, y, lines):
    barrier = pltpu.get_barrier_semaphore()
    me = z * 2 + y

    def call(dev):
        pl.semaphore_signal(barrier, inc=1, device_id={"expert": dev}, device_id_type=MESH)

    call(me + 1 - 2 * y)
    pl.when(z > 0)(lambda: call(me - 2))
    pl.when(z < lines - 1)(lambda: call(me + 2))
    peers = 1 + jnp.where(z > 0, 1, 0) + jnp.where(z < lines - 1, 1, 0)
    pl.semaphore_wait(barrier, peers)


def gather_kernel(lines, *refs):
    n = 3
    own, full = refs[:n], refs[n:2 * n]
    ssem, rsem, lsem = refs[2 * n:]
    me = lax.axis_index("expert")
    z, y = me // 2, me % 2
    partner = me + 1 - 2 * y

    def move(a, way, owner, dev, src=None):
        return pltpu.make_async_remote_copy(
            src_ref=full[a].at[owner] if src is None else src,
            dst_ref=full[a].at[owner],
            send_sem=ssem.at[a, way, owner],
            recv_sem=rsem.at[a, owner],
            device_id={"expert": dev},
            device_id_type=MESH,
        )

    greet(z, y, lines)
    for a in range(n):
        pl.when(z < lines - 1)(lambda: move(a, 0, me, me + 2, own[a]).start())
        pl.when(z > 0)(lambda: move(a, 1, me, me - 2, own[a]).start())
        move(a, 2, me, partner, own[a]).start()
    local = [pltpu.make_async_copy(own[a], full[a].at[me], lsem.at[a]) for a in range(n)]
    for copy in local:
        copy.start()
    for a in range(n):
        for s in range(1, lines):
            @pl.when(z >= s)
            def _():
                owner = me - 2 * s
                move(a, 0, owner, partner).wait_recv()
                pl.when(z < lines - 1)(lambda: move(a, 0, owner, me + 2).start())
                move(a, 2, owner, partner).start()

            @pl.when(z + s < lines)
            def _():
                owner = me + 2 * s
                move(a, 1, owner, partner).wait_recv()
                pl.when(z > 0)(lambda: move(a, 1, owner, me - 2).start())
                move(a, 2, owner, partner).start()
    for a in range(n):
        for line in range(lines):
            move(a, 2, line * 2 + 1 - y, partner).wait_recv()
            move(a, 2, line * 2 + y, partner).wait_send()

            @pl.when((line <= z) & (z < lines - 1))
            def _():
                move(a, 0, line * 2 + y, partner).wait_send()

            @pl.when((line >= z) & (z > 0))
            def _():
                move(a, 1, line * 2 + y, partner).wait_send()
    for copy in local:
        copy.wait()


def all_rows(experts, *blocks):
    n = len(blocks)
    return pl.pallas_call(
        functools.partial(gather_kernel, experts // 2),
        out_shape=[jax.ShapeDtypeStruct((experts,) + b.shape, b.dtype) for b in blocks],
        in_specs=[VM] * n,
        out_specs=[VM] * n,
        scratch_shapes=[
            pltpu.SemaphoreType.DMA((n, 3, experts)),
            pltpu.SemaphoreType.DMA((n, experts)),
            pltpu.SemaphoreType.DMA((n,)),
        ],
        compiler_params=pltpu.CompilerParams(
            collective_id=0, has_side_effects=True, vmem_limit_bytes=40 << 20
        ),
    )(*blocks)


def scatter_kernel(lines, *refs):
    n = 3
    full, out = refs[:n], refs[n:2 * n]
    ybuf, ubuf, dbuf, sbuf = (refs[(2 + i) * n:(3 + i) * n] for i in range(4))
    ysend, yrecv, zsend, urecv, drecv = refs[6 * n:]
    me = lax.axis_index("expert")
    z, y = me // 2, me % 2
    partner = me + 1 - 2 * y

    def across(a, line):
        return pltpu.make_async_remote_copy(
            src_ref=full[a].at[line * 2 + 1 - y],
            dst_ref=ybuf[a].at[line],
            send_sem=ysend.at[a, line],
            recv_sem=yrecv.at[a, line],
            device_id={"expert": partner},
            device_id_type=MESH,
        )

    def along(a, line, up):
        return pltpu.make_async_remote_copy(
            src_ref=sbuf[a].at[line],
            dst_ref=(ubuf if up else dbuf)[a].at[line],
            send_sem=zsend.at[a, line],
            recv_sem=(urecv if up else drecv).at[a, line],
            device_id={"expert": me + 2 if up else me - 2},
            device_id_type=MESH,
        )

    def base(a, line):
        across(a, line).wait_recv()
        return full[a][line * 2 + y].astype(F32) + ybuf[a][line].astype(F32)

    greet(z, y, lines)
    for a in range(n):
        for s in range(lines - 1, 0, -1):
            pl.when(z + s < lines)(lambda: across(a, z + s).start())
            pl.when(z >= s)(lambda: across(a, z - s).start())
        across(a, z).start()
    for a in range(n):
        for s in range(lines - 1, 0, -1):
            @pl.when(z + s < lines)
            def _():
                line = z + s
                sbuf[a][line] = base(a, line).astype(sbuf[a].dtype)

                @pl.when(z > 0)
                def _():
                    along(a, line, True).wait_recv()
                    sbuf[a][line] = (
                        sbuf[a][line].astype(F32) + ubuf[a][line].astype(F32)
                    ).astype(sbuf[a].dtype)

                along(a, line, True).start()

            @pl.when(z >= s)
            def _():
                line = z - s
                sbuf[a][line] = base(a, line).astype(sbuf[a].dtype)

                @pl.when(z < lines - 1)
                def _():
                    along(a, line, False).wait_recv()
                    sbuf[a][line] = (
                        sbuf[a][line].astype(F32) + dbuf[a][line].astype(F32)
                    ).astype(sbuf[a].dtype)

                along(a, line, False).start()
    for a in range(n):
        pl.when(z > 0)(lambda: along(a, z, True).wait_recv())
        pl.when(z < lines - 1)(lambda: along(a, z, False).wait_recv())
        total = base(a, z)
        total = total + jnp.where(z > 0, ubuf[a][z].astype(F32), 0.0)
        total = total + jnp.where(z < lines - 1, dbuf[a][z].astype(F32), 0.0)
        out[a][...] = total.astype(out[a].dtype)
        for line in range(lines):
            across(a, line).wait_send()
            pl.when(z != line)(lambda: along(a, line, True).wait_send())


def sum_rows(experts, *blocks):
    n, lines = len(blocks), experts // 2
    half = [pltpu.VMEM((lines,) + b.shape[1:], b.dtype) for b in blocks]
    return pl.pallas_call(
        functools.partial(scatter_kernel, lines),
        out_shape=[jax.ShapeDtypeStruct(b.shape[1:], b.dtype) for b in blocks],
        in_specs=[VM] * n,
        out_specs=[VM] * n,
        scratch_shapes=half * 4 + [pltpu.SemaphoreType.DMA((n, lines))] * 5,
        compiler_params=pltpu.CompilerParams(
            collective_id=1, has_side_effects=True, vmem_limit_bytes=40 << 20
        ),
    )(*blocks)


def per_device(tokens, routes, gates, w_gate, w_up, w_down, cotangent):
    tok_rows, quarter = tokens.shape
    top_count = routes.shape[1]
    experts = lax.axis_size("expert")
    capacity = max(2, (3 * tok_rows * top_count + 2 * experts - 1) // (2 * experts))
    slots = experts * capacity
    q = slots // 4
    me = lax.axis_index("expert")
    d = lax.axis_index("dp")
    wg, wu, wd = w_gate[0], w_up[0], w_down[0]

    labels = jnp.arange(experts, dtype=jnp.int32)
    chosen = routes[:, :, None] == labels[None, None, :]
    table = jnp.sum(jnp.where(chosen, gates[:, :, None], 0.0), axis=1)
    near = experts == 8
    if near:
        tables, x, c = all_rows(experts, table.T, tokens, cotangent)
        weight = lax.dynamic_index_in_dim(tables, me, axis=1, keepdims=False)
        x = x.reshape(experts * tok_rows, quarter)
        c = c.reshape(experts * tok_rows, quarter)
    else:
        weight = lax.all_to_all(table.T, "expert", split_axis=0, concat_axis=0, tiled=True)
        x = lax.all_gather(tokens, "expert", axis=0, tiled=True)
        c = lax.all_gather(cotangent, "expert", axis=0, tiled=True)
    weight = weight.reshape(experts * tok_rows)

    routed = weight > 0.0
    rank = jnp.cumsum(routed.astype(jnp.int32)) - 1
    rank = jnp.where(routed, rank, -1)
    place = jnp.arange(slots, dtype=jnp.int32)
    place = (place // q ^ d) * q + place % q
    hit = place[:, None] == rank[None, :]
    pick = hit.astype(BF)
    slot_gate = jnp.sum(jnp.where(hit, weight[None, :], 0.0), axis=1)

    xs = dot(pick, x).astype(BF)
    gate_pre = reduce_rows(dot(xs, wg).astype(BF))
    up_pre = reduce_rows(dot(xs, wu).astype(BF))
    cs = dot(pick, c).astype(BF)
    raw_grad = reduce_rows(dot_nt(cs, wd).astype(BF))

    own_gate = slot_gate[:q, None]
    sig = jax.nn.sigmoid(gate_pre)
    active = gate_pre * sig
    hidden32 = active * up_pre
    hidden = gather_rows(hidden32.astype(BF))
    gate_inner = jnp.sum(hidden32 * raw_grad, axis=1)
    hidden_grad = raw_grad * own_gate
    gpg = gather_rows((hidden_grad * up_pre * sig * (1.0 + gate_pre * (1.0 - sig))).astype(BF))
    upg = gather_rows((hidden_grad * active).astype(BF))

    out = (dot(hidden, wd) * slot_gate[:, None]).astype(BF)
    out = dot_t(pick, out).astype(BF)
    pair = (dot_nt(gpg, wg) + dot_nt(upg, wu)).astype(BF)
    pair = dot_t(pick, pair).astype(BF)

    inner = gather_rows(gate_inner[:, None])
    inner = jnp.sum(jnp.where(hit, inner, 0.0), axis=0).reshape(experts, tok_rows)
    if near:
        mine = (labels == me)[None, :, None]
        inner, mixed, token_grad = sum_rows(
            experts,
            jnp.where(mine, inner[:, None, :], 0.0),
            out.reshape(experts, tok_rows, quarter),
            pair.reshape(experts, tok_rows, quarter),
        )
    else:
        inner = lax.all_to_all(inner, "expert", split_axis=0, concat_axis=0, tiled=True)
        mixed = lax.psum_scatter(out, "expert", scatter_dimension=0, tiled=True)
        token_grad = lax.psum_scatter(pair, "expert", scatter_dimension=0, tiled=True)
    gate_grad = jnp.sum(jnp.where(chosen, inner.T[:, None, :], 0.0), axis=2)

    w_down_grad = dot_t((hidden.astype(F32) * slot_gate[:, None]).astype(BF), cs).astype(BF)[None]
    w_gate_grad = dot_t(xs, gpg).astype(BF)[None]
    w_up_grad = dot_t(xs, upg).astype(BF)[None]
    return mixed, token_grad, gate_grad, w_gate_grad, w_up_grad, w_down_grad


def solution(mesh):
    placed = (
        P("expert", "dp"),
        P("expert", None),
        P("expert", None),
        P("expert", "dp", None),
        P("expert", "dp", None),
        P("expert", None, "dp"),
        P("expert", "dp"),
    )
    return jax.shard_map(
        per_device,
        mesh=mesh,
        in_specs=placed,
        out_specs=(
            P("expert", "dp"),
            P("expert", "dp"),
            P("expert", None),
            P("expert", "dp", None),
            P("expert", "dp", None),
            P("expert", None, "dp"),
        ),
        check_vma=False,
    )
```

```python
import functools

import jax
import jax.numpy as jnp
from jax import lax
from jax.experimental import pallas as pl
from jax.experimental.pallas import tpu as pltpu
from jax.sharding import PartitionSpec as P

BF = jnp.bfloat16
F32 = jnp.float32


def dot(a, b):
    return jnp.dot(a, b, preferred_element_type=F32)


def dot_t(a, b):
    return lax.dot_general(a, b, (((0,), (0,)), ((), ())), preferred_element_type=F32)


def dot_nt(a, b):
    return lax.dot_general(a, b, (((1,), (1,)), ((), ())), preferred_element_type=F32)


def hop(v, bit):
    count = lax.axis_size("dp")
    return lax.ppermute(v, "dp", [(i, i ^ bit) for i in range(count)])


def reduce_rows(p):
    q = p.shape[0] // 4
    sent = jnp.concatenate([p[q:2 * q], p[3 * q:]], axis=0)
    got = hop(sent, 1)
    kept = p[:q].astype(F32) + got[:q].astype(F32)
    other = (p[2 * q:3 * q].astype(F32) + got[q:].astype(F32)).astype(BF)
    return kept + hop(other, 2).astype(F32)


def gather_rows(h):
    both = jnp.concatenate([h, hop(h, 2)], axis=0)
    far = hop(both, 1)
    q = h.shape[0]
    return jnp.concatenate([both[:q], far[:q], both[q:], far[q:]], axis=0)


MESH = pl.DeviceIdType.MESH
VM = pl.BlockSpec(memory_space=pltpu.VMEM)


def greet(z, y, lines, dp_peers=()):
    barrier = pltpu.get_barrier_semaphore()
    me = z * 2 + y

    def call(**dev):
        pl.semaphore_signal(barrier, inc=1, device_id=dev, device_id_type=MESH)

    call(expert=me + 1 - 2 * y)
    for dev in dp_peers:
        call(dp=dev)
    pl.when(z > 0)(lambda: call(expert=me - 2))
    pl.when(z < lines - 1)(lambda: call(expert=me + 2))
    peers = 1 + len(dp_peers) + jnp.where(z > 0, 1, 0) + jnp.where(z < lines - 1, 1, 0)
    pl.semaphore_wait(barrier, peers)


def rows_dot(out, left, right, contract, rows):
    @pl.loop(0, out.shape[0] // rows)
    def _(i):
        at = pl.ds(pl.multiple_of(i * rows, rows), rows)
        out[at, :] = lax.dot_general(
            left[at, :], right[...], (((1,), (contract,)), ((), ())), preferred_element_type=F32
        ).astype(out.dtype)


def front_kernel(lines, table, tok, cot, wg, wu, wd, hidden, gpg, upg, inner, xs, cs, pick, gate_out,
                 tall, xall, call, part, cbuf, obuf, xbuf, fbuf, ssem, rsem, lsem, cs_sem, cr_sem,
                 xs_sem, xr_sem, gxs, gxr, gcs, gcr):
    own, full = (table, tok, cot), (tall, xall, call)
    me = lax.axis_index("expert")
    d = lax.axis_index("dp")
    z, y = me // 2, me % 2
    xc, cc = d // 2, d % 2
    partner = me + 1 - 2 * y
    core, over = d + 1 - 2 * cc, d + 2 - 4 * xc
    q = inner.shape[1]
    tok_rows = tok.shape[0]
    res = (hidden, gpg, upg)

    def held(a, owner):
        rows = own[a].shape[0]
        return full[a].at[pl.ds(pl.multiple_of(owner * rows, rows), rows)]

    def move(a, way, owner, dev, src=None):
        return pltpu.make_async_remote_copy(
            src_ref=held(a, owner) if src is None else src,
            dst_ref=held(a, owner),
            send_sem=ssem.at[a, way, owner],
            recv_sem=rsem.at[a, owner],
            device_id={"expert": dev},
            device_id_type=MESH,
        )

    def begin(a):
        pl.when(z < lines - 1)(lambda: move(a, 0, me, me + 2, own[a]).start())
        pl.when(z > 0)(lambda: move(a, 1, me, me - 2, own[a]).start())
        move(a, 2, me, partner, own[a]).start()
        pltpu.make_async_copy(own[a], held(a, me), lsem.at[a]).start()

    def forward(a, s):
        @pl.when(z >= s)
        def _():
            owner = me - 2 * s
            move(a, 0, owner, partner).wait_recv()
            pl.when(z < lines - 1)(lambda: move(a, 0, owner, me + 2).start())
            move(a, 2, owner, partner).start()

        @pl.when(z + s < lines)
        def _():
            owner = me + 2 * s
            move(a, 1, owner, partner).wait_recv()
            pl.when(z > 0)(lambda: move(a, 1, owner, me - 2).start())
            move(a, 2, owner, partner).start()

    def arrive(a):
        for line in range(lines):
            move(a, 2, line * 2 + 1 - y, partner).wait_recv()
        pltpu.make_async_copy(own[a], held(a, me), lsem.at[a]).wait()

    def dp_copy(src, dst, send, recv, dev):
        return pltpu.make_async_remote_copy(
            src_ref=src, dst_ref=dst, send_sem=send, recv_sem=recv,
            device_id={"dp": dev}, device_id_type=MESH,
        )

    def to_core(m, i):
        return dp_copy(part.at[m, pl.ds((2 * i + 1) * q, q)], cbuf.at[m, i], cs_sem.at[m, i], cr_sem.at[m, i], core)

    def to_over(m):
        return dp_copy(obuf.at[m], xbuf.at[m], xs_sem.at[m], xr_sem.at[m], over)

    def block(m, i):
        return inner.at[i] if m == 3 else res[m].at[pl.ds(i * q, q)]

    def share_over(m):
        return dp_copy(block(m, 0), block(m, 2), gxs.at[m], gxr.at[m], over)

    def share_core(m, i):
        return dp_copy(block(m, 2 * i), block(m, 2 * i + 1), gcs.at[m, i], gcr.at[m, i], core)

    def send_sum(m):
        for i in range(2):
            to_core(m, i).wait_recv()
        obuf[m] = (part[m, 2 * q:3 * q].astype(F32) + cbuf[m, 1].astype(F32)).astype(BF)
        to_over(m).start()
        fbuf[m] = part[m, :q].astype(F32) + cbuf[m, 0].astype(F32)

    def take_sum(m):
        to_over(m).wait_recv()
        fbuf[m] = fbuf[m] + xbuf[m].astype(F32)

    def share(m):
        share_over(m).start()
        share_core(m, 0).start()

    greet(z, y, lines, (core, over))
    begin(0)
    begin(1)
    for s in range(1, lines):
        forward(0, s)
    arrive(0)
    tables = tall[...].reshape(2 * lines, 2 * lines, tok_rows)
    chosen = lax.broadcasted_iota(jnp.int32, tables.shape, 1) == me
    weight = jnp.sum(jnp.where(chosen, tables, 0.0), axis=1)
    routed = weight > 0.0
    upto = lax.broadcasted_iota(jnp.int32, (tok_rows, tok_rows), 0) <= lax.broadcasted_iota(
        jnp.int32, (tok_rows, tok_rows), 1
    )
    count = jnp.dot(
        jnp.where(routed, 1.0, 0.0), jnp.where(upto, 1.0, 0.0), preferred_element_type=F32
    )
    forward(1, 1)
    begin(2)
    gates = [jnp.zeros((q, 1), F32) for _ in range(4)]
    before = jnp.zeros((1, 1), F32)
    for src in range(2 * lines):
        row = slice(src, src + 1)
        rank = jnp.where(routed[row], count[row] - 1.0 + before, -1.0)
        before = before + count[row, tok_rows - 1:]
        for b in range(4):
            owner = (xc + b // 2) % 2 * 2 + (cc + b % 2) % 2
            ids = (lax.broadcasted_iota(jnp.int32, (q, tok_rows), 0) + owner * q).astype(F32)
            hit = ids == rank
            pick[b * q:(b + 1) * q, src * tok_rows:(src + 1) * tok_rows] = jnp.where(hit, 1.0, 0.0).astype(BF)
            gates[b] = gates[b] + jnp.sum(jnp.where(hit, weight[row], 0.0), axis=1, keepdims=True)
        if src == 3:
            forward(1, 2)
    for b in range(4):
        gate_out[b * q:(b + 1) * q, :] = jnp.broadcast_to(gates[b], (q, 128))
    for s in range(3, lines):
        forward(1, s)
    arrive(1)
    rows_dot(xs, pick, xall, 0, 2 * q)
    forward(2, 1)
    rows_dot(part.at[0], xs, wg, 0, 2 * q)
    for i in range(2):
        to_core(0, i).start()
    forward(2, 2)
    rows_dot(part.at[1], xs, wu, 0, 2 * q)
    for i in range(2):
        to_core(1, i).start()
    send_sum(0)
    send_sum(1)
    for s in range(3, lines):
        forward(2, s)
    take_sum(0)
    take_sum(1)
    gate_pre, up_pre = fbuf[0], fbuf[1]
    hidden[:q, :] = (gate_pre * jax.nn.sigmoid(gate_pre) * up_pre).astype(BF)
    share(0)
    arrive(2)
    rows_dot(cs, pick, call, 0, 2 * q)
    rows_dot(part.at[2], cs, wd, 1, 2 * q)
    for i in range(2):
        to_core(2, i).start()
    send_sum(2)
    share_over(0).wait_recv()
    share_core(0, 1).start()
    take_sum(2)

    gate_pre, up_pre, raw = fbuf[0], fbuf[1], fbuf[2]
    sig = jax.nn.sigmoid(gate_pre)
    active = gate_pre * sig
    grad = raw * gate_out[:q, :1]
    gpg[:q, :] = (grad * up_pre * sig * (1.0 + gate_pre * (1.0 - sig))).astype(BF)
    share(1)
    upg[:q, :] = (grad * active).astype(BF)
    share(2)
    inner[0] = jnp.broadcast_to(jnp.sum(active * up_pre * raw, axis=1, keepdims=True), (q, 128))
    share(3)
    for m in (1, 2, 3):
        share_over(m).wait_recv()
        share_core(m, 1).start()
    for m in range(4):
        for i in range(2):
            share_core(m, i).wait_recv()
    for m in range(4):
        share_over(m).wait_send()
        for i in range(2):
            share_core(m, i).wait_send()
    for m in range(3):
        to_over(m).wait_send()
        for i in range(2):
            to_core(m, i).wait_send()
    for a in range(3):
        for line in range(lines):
            move(a, 2, line * 2 + y, partner).wait_send()

            @pl.when((line <= z) & (z < lines - 1))
            def _():
                move(a, 0, line * 2 + y, partner).wait_send()

            @pl.when((line >= z) & (z > 0))
            def _():
                move(a, 1, line * 2 + y, partner).wait_send()


def front(experts, slots, table, tok, cot, wg, wu, wd):
    tok_rows, quarter = tok.shape
    width, q = wd.shape[0], slots // 4
    sds = jax.ShapeDtypeStruct
    dma = pltpu.SemaphoreType.DMA
    blocks = pltpu.VMEM((3, q, width), BF)
    return pl.pallas_call(
        functools.partial(front_kernel, experts // 2),
        out_shape=[sds((slots, width), BF)] * 3
        + [sds((4, q, 128), F32)]
        + [sds((slots, quarter), BF)] * 2
        + [sds((slots, experts * tok_rows), BF), sds((slots, 128), F32)],
        in_specs=[VM] * 6,
        out_specs=[VM] * 8,
        scratch_shapes=[
            pltpu.VMEM((experts * experts, tok_rows), F32),
            pltpu.VMEM((experts * tok_rows, quarter), BF),
            pltpu.VMEM((experts * tok_rows, quarter), BF),
            pltpu.VMEM((3, slots, width), BF),
            pltpu.VMEM((3, 2, q, width), BF),
            blocks,
            blocks,
            pltpu.VMEM((3, q, width), F32),
            dma((3, 3, experts)),
            dma((3, experts)),
            dma((3,)),
            dma((3, 2)),
            dma((3, 2)),
            dma((3,)),
            dma((3,)),
            dma((4,)),
            dma((4,)),
            dma((4, 2)),
            dma((4, 2)),
        ],
        compiler_params=pltpu.CompilerParams(
            collective_id=0, has_side_effects=True, vmem_limit_bytes=56 << 20
        ),
    )(table, tok, cot, wg, wu, wd)


def scatter_kernel(lines, *refs):
    n = 3
    full, out = refs[:n], refs[n:2 * n]
    ybuf, ubuf, dbuf, sbuf = (refs[(2 + i) * n:(3 + i) * n] for i in range(4))
    ysend, yrecv, zsend, urecv, drecv = refs[6 * n:]
    me = lax.axis_index("expert")
    z, y = me // 2, me % 2
    partner = me + 1 - 2 * y

    def across(a, line):
        return pltpu.make_async_remote_copy(
            src_ref=full[a].at[line * 2 + 1 - y],
            dst_ref=ybuf[a].at[line],
            send_sem=ysend.at[a, line],
            recv_sem=yrecv.at[a, line],
            device_id={"expert": partner},
            device_id_type=MESH,
        )

    def along(a, line, up):
        return pltpu.make_async_remote_copy(
            src_ref=sbuf[a].at[line],
            dst_ref=(ubuf if up else dbuf)[a].at[line],
            send_sem=zsend.at[a, line],
            recv_sem=(urecv if up else drecv).at[a, line],
            device_id={"expert": me + 2 if up else me - 2},
            device_id_type=MESH,
        )

    def base(a, line):
        across(a, line).wait_recv()
        return full[a][line * 2 + y].astype(F32) + ybuf[a][line].astype(F32)

    greet(z, y, lines)
    for a in range(n):
        for s in range(lines - 1, 0, -1):
            pl.when(z + s < lines)(lambda: across(a, z + s).start())
            pl.when(z >= s)(lambda: across(a, z - s).start())
        across(a, z).start()
    for a in range(n):
        for s in range(lines - 1, 0, -1):
            @pl.when(z + s < lines)
            def _():
                line = z + s
                sbuf[a][line] = base(a, line).astype(sbuf[a].dtype)

                @pl.when(z > 0)
                def _():
                    along(a, line, True).wait_recv()
                    sbuf[a][line] = (
                        sbuf[a][line].astype(F32) + ubuf[a][line].astype(F32)
                    ).astype(sbuf[a].dtype)

                along(a, line, True).start()

            @pl.when(z >= s)
            def _():
                line = z - s
                sbuf[a][line] = base(a, line).astype(sbuf[a].dtype)

                @pl.when(z < lines - 1)
                def _():
                    along(a, line, False).wait_recv()
                    sbuf[a][line] = (
                        sbuf[a][line].astype(F32) + dbuf[a][line].astype(F32)
                    ).astype(sbuf[a].dtype)

                along(a, line, False).start()
    for a in range(n):
        pl.when(z > 0)(lambda: along(a, z, True).wait_recv())
        pl.when(z < lines - 1)(lambda: along(a, z, False).wait_recv())
        total = base(a, z)
        total = total + jnp.where(z > 0, ubuf[a][z].astype(F32), 0.0)
        total = total + jnp.where(z < lines - 1, dbuf[a][z].astype(F32), 0.0)
        out[a][...] = total.astype(out[a].dtype)
        for line in range(lines):
            across(a, line).wait_send()
            pl.when(z != line)(lambda: along(a, line, True).wait_send())


def sum_rows(experts, *blocks):
    n, lines = len(blocks), experts // 2
    half = [pltpu.VMEM((lines,) + b.shape[1:], b.dtype) for b in blocks]
    return pl.pallas_call(
        functools.partial(scatter_kernel, lines),
        out_shape=[jax.ShapeDtypeStruct(b.shape[1:], b.dtype) for b in blocks],
        in_specs=[VM] * n,
        out_specs=[VM] * n,
        scratch_shapes=half * 4 + [pltpu.SemaphoreType.DMA((n, lines))] * 5,
        compiler_params=pltpu.CompilerParams(
            collective_id=1, has_side_effects=True, vmem_limit_bytes=40 << 20
        ),
    )(*blocks)


def per_device(tokens, routes, gates, w_gate, w_up, w_down, cotangent):
    tok_rows, quarter = tokens.shape
    top_count = routes.shape[1]
    experts = lax.axis_size("expert")
    capacity = max(2, (3 * tok_rows * top_count + 2 * experts - 1) // (2 * experts))
    slots = experts * capacity
    q = slots // 4
    me = lax.axis_index("expert")
    d = lax.axis_index("dp")
    wg, wu, wd = w_gate[0], w_up[0], w_down[0]

    labels = jnp.arange(experts, dtype=jnp.int32)
    chosen = routes[:, :, None] == labels[None, None, :]
    table = jnp.sum(jnp.where(chosen, gates[:, :, None], 0.0), axis=1)
    near = experts == 8
    if near:
        hidden, gpg, upg, inner, xs, cs, pick, slot_gate = front(
            experts, slots, table.T, tokens, cotangent, wg, wu, wd
        )
        slot_gate = slot_gate[:, 0]
        inner = inner[:, :, :1].reshape(slots, 1)
    else:
        weight = lax.all_to_all(table.T, "expert", split_axis=0, concat_axis=0, tiled=True)
        x = lax.all_gather(tokens, "expert", axis=0, tiled=True)
        c = lax.all_gather(cotangent, "expert", axis=0, tiled=True)
        weight = weight.reshape(experts * tok_rows)

        routed = weight > 0.0
        rank = jnp.cumsum(routed.astype(jnp.int32)) - 1
        rank = jnp.where(routed, rank, -1)
        place = jnp.arange(slots, dtype=jnp.int32)
        place = (place // q ^ d) * q + place % q
        hit = place[:, None] == rank[None, :]
        pick = hit.astype(BF)
        slot_gate = jnp.sum(jnp.where(hit, weight[None, :], 0.0), axis=1)

        xs = dot(pick, x).astype(BF)
        gate_pre = reduce_rows(dot(xs, wg).astype(BF))
        up_pre = reduce_rows(dot(xs, wu).astype(BF))
        cs = dot(pick, c).astype(BF)
        raw_grad = reduce_rows(dot_nt(cs, wd).astype(BF))

        own_gate = slot_gate[:q, None]
        sig = jax.nn.sigmoid(gate_pre)
        active = gate_pre * sig
        hidden32 = active * up_pre
        hidden = gather_rows(hidden32.astype(BF))
        gate_inner = jnp.sum(hidden32 * raw_grad, axis=1)
        hidden_grad = raw_grad * own_gate
        gpg = gather_rows((hidden_grad * up_pre * sig * (1.0 + gate_pre * (1.0 - sig))).astype(BF))
        upg = gather_rows((hidden_grad * active).astype(BF))

        inner = gather_rows(gate_inner[:, None])

    out = (dot(hidden, wd) * slot_gate[:, None]).astype(BF)
    out = dot_t(pick, out).astype(BF)
    pair = (dot_nt(gpg, wg) + dot_nt(upg, wu)).astype(BF)
    pair = dot_t(pick, pair).astype(BF)

    inner = jnp.sum(jnp.where(pick > 0, inner, 0.0), axis=0).reshape(experts, tok_rows)
    if near:
        mine = (labels == me)[None, :, None]
        inner, mixed, token_grad = sum_rows(
            experts,
            jnp.where(mine, inner[:, None, :], 0.0),
            out.reshape(experts, tok_rows, quarter),
            pair.reshape(experts, tok_rows, quarter),
        )
    else:
        inner = lax.all_to_all(inner, "expert", split_axis=0, concat_axis=0, tiled=True)
        mixed = lax.psum_scatter(out, "expert", scatter_dimension=0, tiled=True)
        token_grad = lax.psum_scatter(pair, "expert", scatter_dimension=0, tiled=True)
    gate_grad = jnp.sum(jnp.where(chosen, inner.T[:, None, :], 0.0), axis=2)

    w_down_grad = dot_t((hidden.astype(F32) * slot_gate[:, None]).astype(BF), cs).astype(BF)[None]
    w_gate_grad = dot_t(xs, gpg).astype(BF)[None]
    w_up_grad = dot_t(xs, upg).astype(BF)[None]
    return mixed, token_grad, gate_grad, w_gate_grad, w_up_grad, w_down_grad


def solution(mesh):
    placed = (
        P("expert", "dp"),
        P("expert", None),
        P("expert", None),
        P("expert", "dp", None),
        P("expert", "dp", None),
        P("expert", None, "dp"),
        P("expert", "dp"),
    )
    return jax.shard_map(
        per_device,
        mesh=mesh,
        in_specs=placed,
        out_specs=(
            P("expert", "dp"),
            P("expert", "dp"),
            P("expert", None),
            P("expert", "dp", None),
            P("expert", "dp", None),
            P("expert", None, "dp"),
        ),
        check_vma=False,
    )
```

```python
import functools

import jax
import jax.numpy as jnp
from jax import lax
from jax.experimental import pallas as pl
from jax.experimental.pallas import tpu as pltpu
from jax.sharding import PartitionSpec as P

BF = jnp.bfloat16
F32 = jnp.float32


def dot(a, b):
    return jnp.dot(a, b, preferred_element_type=F32)


def dot_t(a, b):
    return lax.dot_general(a, b, (((0,), (0,)), ((), ())), preferred_element_type=F32)


def dot_nt(a, b):
    return lax.dot_general(a, b, (((1,), (1,)), ((), ())), preferred_element_type=F32)


def hop(v, bit):
    count = lax.axis_size("dp")
    return lax.ppermute(v, "dp", [(i, i ^ bit) for i in range(count)])


def reduce_rows(p):
    q = p.shape[0] // 4
    sent = jnp.concatenate([p[q:2 * q], p[3 * q:]], axis=0)
    got = hop(sent, 1)
    kept = p[:q].astype(F32) + got[:q].astype(F32)
    other = (p[2 * q:3 * q].astype(F32) + got[q:].astype(F32)).astype(BF)
    return kept + hop(other, 2).astype(F32)


def gather_rows(h):
    both = jnp.concatenate([h, hop(h, 2)], axis=0)
    far = hop(both, 1)
    q = h.shape[0]
    return jnp.concatenate([both[:q], far[:q], both[q:], far[q:]], axis=0)


MESH = pl.DeviceIdType.MESH
VM = pl.BlockSpec(memory_space=pltpu.VMEM)


def greet(z, y, lines, dp_peers=()):
    barrier = pltpu.get_barrier_semaphore()
    me = z * 2 + y

    def call(**dev):
        pl.semaphore_signal(barrier, inc=1, device_id=dev, device_id_type=MESH)

    call(expert=me + 1 - 2 * y)
    for dev in dp_peers:
        call(dp=dev)
    pl.when(z > 0)(lambda: call(expert=me - 2))
    pl.when(z < lines - 1)(lambda: call(expert=me + 2))
    peers = 1 + len(dp_peers) + jnp.where(z > 0, 1, 0) + jnp.where(z < lines - 1, 1, 0)
    pl.semaphore_wait(barrier, peers)


def rows_dot(out, left, right, contract, rows):
    @pl.loop(0, out.shape[0] // rows)
    def _(i):
        at = pl.ds(pl.multiple_of(i * rows, rows), rows)
        out[at, :] = lax.dot_general(
            left[at, :], right[...], (((1,), (contract,)), ((), ())), preferred_element_type=F32
        ).astype(out.dtype)


def cols_dot(out, left, right, cuts):
    for lo, hi in cuts:
        out[lo:hi, :] = lax.dot_general(
            left[:, lo:hi], right[...], (((0,), (0,)), ((), ())), preferred_element_type=F32
        ).astype(out.dtype)


def halves(width):
    cut = (width // 2 + 127) // 128 * 128
    return ((0, cut), (cut, width))


def layer_kernel(lines, table, tok, cot, wg, wu, wd, inner_out, mixed, token_grad, wg_grad, wu_grad, wd_grad,
                 hidden, gpg, upg, inner, xs, cs, pick, gate_out,
                 tall, xall, call, part, cbuf, obuf, xbuf, fbuf, mid, scaled, inner_all, out_all, pair_all,
                 yb0, yb1, yb2, ub0, ub1, ub2, db0, db1, db2, sb0, sb1, sb2,
                 ssem, rsem, lsem, cs_sem, cr_sem,
                 xs_sem, xr_sem, gxs, gxr, gcs, gcr, ysend, yrecv, zsend, urecv, drecv):
    dense, out = (inner_all, out_all, pair_all), (inner_out, mixed, token_grad)
    ybuf, ubuf, dbuf, sbuf = (yb0, yb1, yb2), (ub0, ub1, ub2), (db0, db1, db2), (sb0, sb1, sb2)
    own, full = (table, tok, cot), (tall, xall, call)
    me = lax.axis_index("expert")
    d = lax.axis_index("dp")
    z, y = me // 2, me % 2
    xc, cc = d // 2, d % 2
    partner = me + 1 - 2 * y
    core, over = d + 1 - 2 * cc, d + 2 - 4 * xc
    q = inner.shape[1]
    tok_rows = tok.shape[0]
    res = (hidden, gpg, upg)

    def held(a, owner):
        rows = own[a].shape[0]
        return full[a].at[pl.ds(pl.multiple_of(owner * rows, rows), rows)]

    def move(a, way, owner, dev, src=None):
        return pltpu.make_async_remote_copy(
            src_ref=held(a, owner) if src is None else src,
            dst_ref=held(a, owner),
            send_sem=ssem.at[a, way, owner],
            recv_sem=rsem.at[a, owner],
            device_id={"expert": dev},
            device_id_type=MESH,
        )

    def begin(a):
        pl.when(z < lines - 1)(lambda: move(a, 0, me, me + 2, own[a]).start())
        pl.when(z > 0)(lambda: move(a, 1, me, me - 2, own[a]).start())
        move(a, 2, me, partner, own[a]).start()
        pltpu.make_async_copy(own[a], held(a, me), lsem.at[a]).start()

    def forward(a, s):
        @pl.when(z >= s)
        def _():
            owner = me - 2 * s
            move(a, 0, owner, partner).wait_recv()
            pl.when(z < lines - 1)(lambda: move(a, 0, owner, me + 2).start())
            move(a, 2, owner, partner).start()

        @pl.when(z + s < lines)
        def _():
            owner = me + 2 * s
            move(a, 1, owner, partner).wait_recv()
            pl.when(z > 0)(lambda: move(a, 1, owner, me - 2).start())
            move(a, 2, owner, partner).start()

    def arrive(a):
        for line in range(lines):
            move(a, 2, line * 2 + 1 - y, partner).wait_recv()
        pltpu.make_async_copy(own[a], held(a, me), lsem.at[a]).wait()

    def dp_copy(src, dst, send, recv, dev):
        return pltpu.make_async_remote_copy(
            src_ref=src, dst_ref=dst, send_sem=send, recv_sem=recv,
            device_id={"dp": dev}, device_id_type=MESH,
        )

    def to_core(m, i):
        return dp_copy(part.at[m, pl.ds((2 * i + 1) * q, q)], cbuf.at[m, i], cs_sem.at[m, i], cr_sem.at[m, i], core)

    def to_over(m):
        return dp_copy(obuf.at[m], xbuf.at[m], xs_sem.at[m], xr_sem.at[m], over)

    def block(m, i):
        return inner.at[i] if m == 3 else res[m].at[pl.ds(i * q, q)]

    def share_over(m):
        return dp_copy(block(m, 0), block(m, 2), gxs.at[m], gxr.at[m], over)

    def share_core(m, i):
        return dp_copy(block(m, 2 * i), block(m, 2 * i + 1), gcs.at[m, i], gcr.at[m, i], core)

    def send_sum(m):
        for i in range(2):
            to_core(m, i).wait_recv()
        obuf[m] = (part[m, 2 * q:3 * q].astype(F32) + cbuf[m, 1].astype(F32)).astype(BF)
        to_over(m).start()
        fbuf[m] = part[m, :q].astype(F32) + cbuf[m, 0].astype(F32)

    def take_sum(m):
        to_over(m).wait_recv()
        fbuf[m] = fbuf[m] + xbuf[m].astype(F32)

    def share(m):
        share_over(m).start()
        share_core(m, 0).start()

    def chunk(a, owner):
        rows = out[a].shape[0]
        return pl.ds(pl.multiple_of(owner * rows, rows), rows)

    def across(a, line):
        return pltpu.make_async_remote_copy(
            src_ref=dense[a].at[chunk(a, line * 2 + 1 - y)],
            dst_ref=ybuf[a].at[line],
            send_sem=ysend.at[a, line],
            recv_sem=yrecv.at[a, line],
            device_id={"expert": partner},
            device_id_type=MESH,
        )

    def along(a, line, up):
        return pltpu.make_async_remote_copy(
            src_ref=sbuf[a].at[line],
            dst_ref=(ubuf if up else dbuf)[a].at[line],
            send_sem=zsend.at[a, line],
            recv_sem=(urecv if up else drecv).at[a, line],
            device_id={"expert": me + 2 if up else me - 2},
            device_id_type=MESH,
        )

    def base(a, line):
        across(a, line).wait_recv()
        return dense[a][chunk(a, line * 2 + y), :].astype(F32) + ybuf[a][line].astype(F32)

    def return_begin(a):
        for s in range(lines - 1, 0, -1):
            pl.when(z + s < lines)(lambda: across(a, z + s).start())
            pl.when(z >= s)(lambda: across(a, z - s).start())
        across(a, z).start()

    def return_step(a, s):
        @pl.when(z + s < lines)
        def _():
            line = z + s
            sbuf[a][line] = base(a, line).astype(sbuf[a].dtype)

            @pl.when(z > 0)
            def _():
                along(a, line, True).wait_recv()
                sbuf[a][line] = (
                    sbuf[a][line].astype(F32) + ubuf[a][line].astype(F32)
                ).astype(sbuf[a].dtype)

            along(a, line, True).start()

        @pl.when(z >= s)
        def _():
            line = z - s
            sbuf[a][line] = base(a, line).astype(sbuf[a].dtype)

            @pl.when(z < lines - 1)
            def _():
                along(a, line, False).wait_recv()
                sbuf[a][line] = (
                    sbuf[a][line].astype(F32) + dbuf[a][line].astype(F32)
                ).astype(sbuf[a].dtype)

            along(a, line, False).start()

    def return_end(a):
        pl.when(z > 0)(lambda: along(a, z, True).wait_recv())
        pl.when(z < lines - 1)(lambda: along(a, z, False).wait_recv())
        total = base(a, z)
        total = total + jnp.where(z > 0, ubuf[a][z].astype(F32), 0.0)
        total = total + jnp.where(z < lines - 1, dbuf[a][z].astype(F32), 0.0)
        out[a][...] = total.astype(out[a].dtype)
        for line in range(lines):
            across(a, line).wait_send()
            pl.when(z != line)(lambda: along(a, line, True).wait_send())

    def nt(left, right):
        return lax.dot_general(left, right, (((1,), (1,)), ((), ())), preferred_element_type=F32)

    greet(z, y, lines, (core, over))
    begin(0)
    begin(1)
    for s in range(1, lines):
        forward(0, s)
    arrive(0)
    tables = tall[...].reshape(2 * lines, 2 * lines, tok_rows)
    chosen = lax.broadcasted_iota(jnp.int32, tables.shape, 1) == me
    weight = jnp.sum(jnp.where(chosen, tables, 0.0), axis=1)
    routed = weight > 0.0
    upto = lax.broadcasted_iota(jnp.int32, (tok_rows, tok_rows), 0) <= lax.broadcasted_iota(
        jnp.int32, (tok_rows, tok_rows), 1
    )
    count = jnp.dot(
        jnp.where(routed, 1.0, 0.0), jnp.where(upto, 1.0, 0.0), preferred_element_type=F32
    )
    forward(1, 1)
    begin(2)
    gates = [jnp.zeros((q, 1), F32) for _ in range(4)]
    before = jnp.zeros((1, 1), F32)
    for src in range(2 * lines):
        row = slice(src, src + 1)
        rank = jnp.where(routed[row], count[row] - 1.0 + before, -1.0)
        before = before + count[row, tok_rows - 1:]
        for b in range(4):
            owner = (xc + b // 2) % 2 * 2 + (cc + b % 2) % 2
            ids = (lax.broadcasted_iota(jnp.int32, (q, tok_rows), 0) + owner * q).astype(F32)
            hit = ids == rank
            pick[b * q:(b + 1) * q, src * tok_rows:(src + 1) * tok_rows] = jnp.where(hit, 1.0, 0.0).astype(BF)
            gates[b] = gates[b] + jnp.sum(jnp.where(hit, weight[row], 0.0), axis=1, keepdims=True)
        if src == 3:
            forward(1, 2)
    for b in range(4):
        gate_out[b * q:(b + 1) * q, :] = jnp.broadcast_to(gates[b], (q, 128))
    for s in range(3, lines):
        forward(1, s)
    arrive(1)
    rows_dot(xs, pick, xall, 0, 2 * q)
    forward(2, 1)
    rows_dot(part.at[0], xs, wg, 0, 2 * q)
    for i in range(2):
        to_core(0, i).start()
    forward(2, 2)
    rows_dot(part.at[1], xs, wu, 0, 2 * q)
    for i in range(2):
        to_core(1, i).start()
    send_sum(0)
    send_sum(1)
    for s in range(3, lines):
        forward(2, s)
    take_sum(0)
    take_sum(1)
    gate_pre, up_pre = fbuf[0], fbuf[1]
    hidden[:q, :] = (gate_pre * jax.nn.sigmoid(gate_pre) * up_pre).astype(BF)
    share(0)
    arrive(2)
    rows_dot(cs, pick, call, 0, 2 * q)
    rows_dot(part.at[2], cs, wd, 1, 2 * q)
    for i in range(2):
        to_core(2, i).start()
    send_sum(2)

    def finish(m):
        share_over(m).wait_recv()
        share_core(m, 1).start()

    def whole(m):
        for i in range(2):
            share_core(m, i).wait_recv()

    finish(0)
    whole(0)

    @pl.loop(0, 2)
    def _(i):
        at = pl.ds(pl.multiple_of(i * 2 * q, 2 * q), 2 * q)
        mid[at, :] = (
            jnp.dot(hidden[at, :], wd[...], preferred_element_type=F32) * gate_out[at, :1]
        ).astype(BF)
        scaled[at, :] = (hidden[at, :].astype(F32) * gate_out[at, :1]).astype(BF)

    cols_dot(out_all, pick, mid, halves(pick.shape[1]))
    return_begin(1)
    take_sum(2)

    gate_pre, up_pre, raw = fbuf[0], fbuf[1], fbuf[2]
    sig = jax.nn.sigmoid(gate_pre)
    active = gate_pre * sig
    grad = raw * gate_out[:q, :1]
    gpg[:q, :] = (grad * up_pre * sig * (1.0 + gate_pre * (1.0 - sig))).astype(BF)
    share(1)
    upg[:q, :] = (grad * active).astype(BF)
    share(2)
    inner[0] = jnp.broadcast_to(jnp.sum(active * up_pre * raw, axis=1, keepdims=True), (q, 128))
    share(3)
    cols_dot(wd_grad, scaled, cs, halves(scaled.shape[1]))
    return_step(1, lines - 1)
    finish(1)
    for s in range(lines - 2, 0, -1):
        return_step(1, s)
    finish(2)
    finish(3)
    whole(1)
    whole(2)

    @pl.loop(0, 2)
    def _(i):
        at = pl.ds(pl.multiple_of(i * 2 * q, 2 * q), 2 * q)
        mid[at, :] = (nt(gpg[at, :], wg[...]) + nt(upg[at, :], wu[...])).astype(BF)

    cols_dot(pair_all, pick, mid, halves(pick.shape[1]))
    return_begin(2)
    whole(3)
    sums = jnp.zeros((1, pick.shape[1]), F32)
    for b in range(4):
        sums = sums + jnp.sum(
            pick[b * q:(b + 1) * q, :].astype(F32) * inner[b][:, :1], axis=0, keepdims=True
        )
    for dst in range(2 * lines):
        row = sums[:, dst * tok_rows:(dst + 1) * tok_rows]
        mine = lax.broadcasted_iota(jnp.int32, (2 * lines, tok_rows), 0) == me
        inner_all[dst * 2 * lines:(dst + 1) * 2 * lines, :] = jnp.where(mine, row, 0.0)
    return_begin(0)
    cols_dot(wg_grad, xs, gpg, halves(xs.shape[1]))
    for s in range(lines - 1, 0, -1):
        return_step(2, s)
        return_step(0, s)
        if s == lines - 1:
            cols_dot(wu_grad, xs, upg, halves(xs.shape[1]))
    return_end(1)
    return_end(0)
    return_end(2)
    for m in range(4):
        share_over(m).wait_send()
        for i in range(2):
            share_core(m, i).wait_send()
    for m in range(3):
        to_over(m).wait_send()
        for i in range(2):
            to_core(m, i).wait_send()
    for a in range(3):
        for line in range(lines):
            move(a, 2, line * 2 + y, partner).wait_send()

            @pl.when((line <= z) & (z < lines - 1))
            def _():
                move(a, 0, line * 2 + y, partner).wait_send()

            @pl.when((line >= z) & (z > 0))
            def _():
                move(a, 1, line * 2 + y, partner).wait_send()


def layer(experts, slots, table, tok, cot, wg, wu, wd):
    tok_rows, quarter = tok.shape
    width, q = wd.shape[0], slots // 4
    half = [pltpu.VMEM((experts // 2,) + b.shape, b.dtype) for b in (table, tok, tok)]
    sds = jax.ShapeDtypeStruct
    dma = pltpu.SemaphoreType.DMA
    blocks = pltpu.VMEM((3, q, width), BF)
    return pl.pallas_call(
        functools.partial(layer_kernel, experts // 2),
        out_shape=[sds(table.shape, F32), sds(tok.shape, BF), sds(tok.shape, BF)]
        + [sds(w.shape, BF) for w in (wg, wu, wd)],
        in_specs=[VM] * 6,
        out_specs=[VM] * 6,
        scratch_shapes=[
            pltpu.VMEM((slots, width), BF),
            pltpu.VMEM((slots, width), BF),
            pltpu.VMEM((slots, width), BF),
            pltpu.VMEM((4, q, 128), F32),
            pltpu.VMEM((slots, quarter), BF),
            pltpu.VMEM((slots, quarter), BF),
            pltpu.VMEM((slots, experts * tok_rows), BF),
            pltpu.VMEM((slots, 128), F32),
            pltpu.VMEM((experts * experts, tok_rows), F32),
            pltpu.VMEM((experts * tok_rows, quarter), BF),
            pltpu.VMEM((experts * tok_rows, quarter), BF),
            pltpu.VMEM((3, slots, width), BF),
            pltpu.VMEM((3, 2, q, width), BF),
            blocks,
            blocks,
            pltpu.VMEM((3, q, width), F32),
            pltpu.VMEM((slots, quarter), BF),
            pltpu.VMEM((slots, width), BF),
            pltpu.VMEM((experts * experts, tok_rows), F32),
            pltpu.VMEM((experts * tok_rows, quarter), BF),
            pltpu.VMEM((experts * tok_rows, quarter), BF),
        ]
        + half * 4
        + [
            dma((3, 3, experts)),
            dma((3, experts)),
            dma((3,)),
            dma((3, 2)),
            dma((3, 2)),
            dma((3,)),
            dma((3,)),
            dma((4,)),
            dma((4,)),
            dma((4, 2)),
            dma((4, 2)),
        ]
        + [dma((3, experts // 2))] * 5,
        compiler_params=pltpu.CompilerParams(
            collective_id=0, has_side_effects=True, vmem_limit_bytes=60 << 20
        ),
    )(table, tok, cot, wg, wu, wd)


def per_device(tokens, routes, gates, w_gate, w_up, w_down, cotangent):
    tok_rows, quarter = tokens.shape
    top_count = routes.shape[1]
    experts = lax.axis_size("expert")
    capacity = max(2, (3 * tok_rows * top_count + 2 * experts - 1) // (2 * experts))
    slots = experts * capacity
    q = slots // 4
    me = lax.axis_index("expert")
    d = lax.axis_index("dp")
    wg, wu, wd = w_gate[0], w_up[0], w_down[0]

    labels = jnp.arange(experts, dtype=jnp.int32)
    chosen = routes[:, :, None] == labels[None, None, :]
    table = jnp.sum(jnp.where(chosen, gates[:, :, None], 0.0), axis=1)
    near = experts == 8
    if near:
        inner, mixed, token_grad, w_gate_grad, w_up_grad, w_down_grad = layer(
            experts, slots, table.T, tokens, cotangent, wg, wu, wd
        )
        gate_grad = jnp.sum(jnp.where(chosen, inner.T[:, None, :], 0.0), axis=2)
        return mixed, token_grad, gate_grad, w_gate_grad[None], w_up_grad[None], w_down_grad[None]
    weight = lax.all_to_all(table.T, "expert", split_axis=0, concat_axis=0, tiled=True)
    x = lax.all_gather(tokens, "expert", axis=0, tiled=True)
    c = lax.all_gather(cotangent, "expert", axis=0, tiled=True)
    weight = weight.reshape(experts * tok_rows)

    routed = weight > 0.0
    rank = jnp.cumsum(routed.astype(jnp.int32)) - 1
    rank = jnp.where(routed, rank, -1)
    place = jnp.arange(slots, dtype=jnp.int32)
    place = (place // q ^ d) * q + place % q
    hit = place[:, None] == rank[None, :]
    pick = hit.astype(BF)
    slot_gate = jnp.sum(jnp.where(hit, weight[None, :], 0.0), axis=1)

    xs = dot(pick, x).astype(BF)
    gate_pre = reduce_rows(dot(xs, wg).astype(BF))
    up_pre = reduce_rows(dot(xs, wu).astype(BF))
    cs = dot(pick, c).astype(BF)
    raw_grad = reduce_rows(dot_nt(cs, wd).astype(BF))

    own_gate = slot_gate[:q, None]
    sig = jax.nn.sigmoid(gate_pre)
    active = gate_pre * sig
    hidden32 = active * up_pre
    hidden = gather_rows(hidden32.astype(BF))
    gate_inner = jnp.sum(hidden32 * raw_grad, axis=1)
    hidden_grad = raw_grad * own_gate
    gpg = gather_rows((hidden_grad * up_pre * sig * (1.0 + gate_pre * (1.0 - sig))).astype(BF))
    upg = gather_rows((hidden_grad * active).astype(BF))

    inner = gather_rows(gate_inner[:, None])

    out = (dot(hidden, wd) * slot_gate[:, None]).astype(BF)
    out = dot_t(pick, out).astype(BF)
    pair = (dot_nt(gpg, wg) + dot_nt(upg, wu)).astype(BF)
    pair = dot_t(pick, pair).astype(BF)

    inner = jnp.sum(jnp.where(pick > 0, inner, 0.0), axis=0).reshape(experts, tok_rows)
    inner = lax.all_to_all(inner, "expert", split_axis=0, concat_axis=0, tiled=True)
    mixed = lax.psum_scatter(out, "expert", scatter_dimension=0, tiled=True)
    token_grad = lax.psum_scatter(pair, "expert", scatter_dimension=0, tiled=True)
    gate_grad = jnp.sum(jnp.where(chosen, inner.T[:, None, :], 0.0), axis=2)

    w_down_grad = dot_t((hidden.astype(F32) * slot_gate[:, None]).astype(BF), cs).astype(BF)[None]
    w_gate_grad = dot_t(xs, gpg).astype(BF)[None]
    w_up_grad = dot_t(xs, upg).astype(BF)[None]
    return mixed, token_grad, gate_grad, w_gate_grad, w_up_grad, w_down_grad


def solution(mesh):
    placed = (
        P("expert", "dp"),
        P("expert", None),
        P("expert", None),
        P("expert", "dp", None),
        P("expert", "dp", None),
        P("expert", None, "dp"),
        P("expert", "dp"),
    )
    return jax.shard_map(
        per_device,
        mesh=mesh,
        in_specs=placed,
        out_specs=(
            P("expert", "dp"),
            P("expert", "dp"),
            P("expert", None),
            P("expert", "dp", None),
            P("expert", "dp", None),
            P("expert", None, "dp"),
        ),
        check_vma=False,
    )
```

```python
import functools

import jax
import jax.numpy as jnp
from jax import lax
from jax.experimental import pallas as pl
from jax.experimental.pallas import tpu as pltpu
from jax.sharding import PartitionSpec as P

BF = jnp.bfloat16
F32 = jnp.float32


def dot(a, b):
    return jnp.dot(a, b, preferred_element_type=F32)


def dot_t(a, b):
    return lax.dot_general(a, b, (((0,), (0,)), ((), ())), preferred_element_type=F32)


def dot_nt(a, b):
    return lax.dot_general(a, b, (((1,), (1,)), ((), ())), preferred_element_type=F32)


def hop(v, bit):
    count = lax.axis_size("dp")
    return lax.ppermute(v, "dp", [(i, i ^ bit) for i in range(count)])


def reduce_rows(p):
    q = p.shape[0] // 4
    sent = jnp.concatenate([p[q:2 * q], p[3 * q:]], axis=0)
    got = hop(sent, 1)
    kept = p[:q].astype(F32) + got[:q].astype(F32)
    other = (p[2 * q:3 * q].astype(F32) + got[q:].astype(F32)).astype(BF)
    return kept + hop(other, 2).astype(F32)


def gather_rows(h):
    both = jnp.concatenate([h, hop(h, 2)], axis=0)
    far = hop(both, 1)
    q = h.shape[0]
    return jnp.concatenate([both[:q], far[:q], both[q:], far[q:]], axis=0)


MESH = pl.DeviceIdType.MESH
VM = pl.BlockSpec(memory_space=pltpu.VMEM)


def greet(z, y, lines, dp_peers=()):
    barrier = pltpu.get_barrier_semaphore()
    me = z * 2 + y

    def call(**dev):
        pl.semaphore_signal(barrier, inc=1, device_id=dev, device_id_type=MESH)

    call(expert=me + 1 - 2 * y)
    for dev in dp_peers:
        call(dp=dev)
    pl.when(z > 0)(lambda: call(expert=me - 2))
    pl.when(z < lines - 1)(lambda: call(expert=me + 2))
    peers = 1 + len(dp_peers) + jnp.where(z > 0, 1, 0) + jnp.where(z < lines - 1, 1, 0)
    pl.semaphore_wait(barrier, peers)


def rows_dot(out, left, right, contract, rows):
    @pl.loop(0, out.shape[0] // rows)
    def _(i):
        at = pl.ds(pl.multiple_of(i * rows, rows), rows)
        out[at, :] = lax.dot_general(
            left[at, :], right[...], (((1,), (contract,)), ((), ())), preferred_element_type=F32
        ).astype(out.dtype)


def cols_dot(out, left, right, cuts):
    for lo, hi in cuts:
        out[lo:hi, :] = lax.dot_general(
            left[:, lo:hi], right[...], (((0,), (0,)), ((), ())), preferred_element_type=F32
        ).astype(out.dtype)


def halves(width):
    cut = (width // 2 + 127) // 128 * 128
    return ((0, cut), (cut, width))


def layer_kernel(lines, table, tok, cot, wg, wu, wd, inner_out, mixed, token_grad, wg_grad, wu_grad, wd_grad,
                 hidden, gpg, upg, inner, xs, cs, pick, gate_out,
                 tall, xall, call, part, cbuf, obuf, xbuf, fbuf, mid, scaled, inner_all, out_all, pair_all,
                 yb0, yb1, yb2, ub0, ub1, ub2, db0, db1, db2, sb0, sb1, sb2,
                 ssem, rsem, lsem, cs_sem, cr_sem,
                 xs_sem, xr_sem, gxs, gxr, gcs, gcr, ysend, yrecv, zsend, urecv, drecv):
    dense, out = (inner_all, out_all, pair_all), (inner_out, mixed, token_grad)
    ybuf, ubuf, dbuf, sbuf = (yb0, yb1, yb2), (ub0, ub1, ub2), (db0, db1, db2), (sb0, sb1, sb2)
    own, full = (table, tok, cot), (tall, xall, call)
    me = lax.axis_index("expert")
    d = lax.axis_index("dp")
    z, y = me // 2, me % 2
    xc, cc = d // 2, d % 2
    partner = me + 1 - 2 * y
    core, over = d + 1 - 2 * cc, d + 2 - 4 * xc
    q = inner.shape[1]
    tok_rows = tok.shape[0]
    res = (hidden, gpg, upg)

    def held(a, owner):
        rows = own[a].shape[0]
        return full[a].at[pl.ds(pl.multiple_of(owner * rows, rows), rows)]

    def move(a, way, owner, dev, src=None):
        return pltpu.make_async_remote_copy(
            src_ref=held(a, owner) if src is None else src,
            dst_ref=held(a, owner),
            send_sem=ssem.at[a, way, owner],
            recv_sem=rsem.at[a, owner],
            device_id={"expert": dev},
            device_id_type=MESH,
        )

    def begin(a):
        pl.when(z < lines - 1)(lambda: move(a, 0, me, me + 2, own[a]).start())
        pl.when(z > 0)(lambda: move(a, 1, me, me - 2, own[a]).start())
        move(a, 2, me, partner, own[a]).start()
        pltpu.make_async_copy(own[a], held(a, me), lsem.at[a]).start()

    def forward(a, s):
        @pl.when(z >= s)
        def _():
            owner = me - 2 * s
            move(a, 0, owner, partner).wait_recv()
            pl.when(z < lines - 1)(lambda: move(a, 0, owner, me + 2).start())
            move(a, 2, owner, partner).start()

        @pl.when(z + s < lines)
        def _():
            owner = me + 2 * s
            move(a, 1, owner, partner).wait_recv()
            pl.when(z > 0)(lambda: move(a, 1, owner, me - 2).start())
            move(a, 2, owner, partner).start()

    def arrive(a):
        for line in range(lines):
            move(a, 2, line * 2 + 1 - y, partner).wait_recv()
        pltpu.make_async_copy(own[a], held(a, me), lsem.at[a]).wait()

    def dp_copy(src, dst, send, recv, dev):
        return pltpu.make_async_remote_copy(
            src_ref=src, dst_ref=dst, send_sem=send, recv_sem=recv,
            device_id={"dp": dev}, device_id_type=MESH,
        )

    def to_core(m, i):
        return dp_copy(part.at[m, pl.ds((2 * i + 1) * q, q)], cbuf.at[m, i], cs_sem.at[m, i], cr_sem.at[m, i], core)

    def to_over(m):
        return dp_copy(obuf.at[m], xbuf.at[m], xs_sem.at[m], xr_sem.at[m], over)

    def block(m, i):
        return inner.at[i] if m == 3 else res[m].at[pl.ds(i * q, q)]

    def share_over(m):
        return dp_copy(block(m, 0), block(m, 2), gxs.at[m], gxr.at[m], over)

    def share_core(m, i):
        return dp_copy(block(m, 2 * i), block(m, 2 * i + 1), gcs.at[m, i], gcr.at[m, i], core)

    def send_sum(m):
        for i in range(2):
            to_core(m, i).wait_recv()
        obuf[m] = (part[m, 2 * q:3 * q].astype(F32) + cbuf[m, 1].astype(F32)).astype(BF)
        to_over(m).start()
        fbuf[m] = part[m, :q].astype(F32) + cbuf[m, 0].astype(F32)

    def take_sum(m):
        to_over(m).wait_recv()
        fbuf[m] = fbuf[m] + xbuf[m].astype(F32)

    def share(m):
        share_over(m).start()
        share_core(m, 0).start()

    def chunk(a, owner):
        rows = out[a].shape[0]
        return pl.ds(pl.multiple_of(owner * rows, rows), rows)

    def across(a, line):
        return pltpu.make_async_remote_copy(
            src_ref=dense[a].at[chunk(a, line * 2 + 1 - y)],
            dst_ref=ybuf[a].at[line],
            send_sem=ysend.at[a, line],
            recv_sem=yrecv.at[a, line],
            device_id={"expert": partner},
            device_id_type=MESH,
        )

    def along(a, line, up):
        return pltpu.make_async_remote_copy(
            src_ref=sbuf[a].at[line],
            dst_ref=(ubuf if up else dbuf)[a].at[line],
            send_sem=zsend.at[a, line],
            recv_sem=(urecv if up else drecv).at[a, line],
            device_id={"expert": me + 2 if up else me - 2},
            device_id_type=MESH,
        )

    def base(a, line):
        across(a, line).wait_recv()
        return dense[a][chunk(a, line * 2 + y), :].astype(F32) + ybuf[a][line].astype(F32)

    def return_begin(a):
        for s in range(lines - 1, 0, -1):
            pl.when(z + s < lines)(lambda: across(a, z + s).start())
            pl.when(z >= s)(lambda: across(a, z - s).start())
        across(a, z).start()

    def return_step(a, s):
        @pl.when(z + s < lines)
        def _():
            line = z + s
            sbuf[a][line] = base(a, line).astype(sbuf[a].dtype)

            @pl.when(z > 0)
            def _():
                along(a, line, True).wait_recv()
                sbuf[a][line] = (
                    sbuf[a][line].astype(F32) + ubuf[a][line].astype(F32)
                ).astype(sbuf[a].dtype)

            along(a, line, True).start()

        @pl.when(z >= s)
        def _():
            line = z - s
            sbuf[a][line] = base(a, line).astype(sbuf[a].dtype)

            @pl.when(z < lines - 1)
            def _():
                along(a, line, False).wait_recv()
                sbuf[a][line] = (
                    sbuf[a][line].astype(F32) + dbuf[a][line].astype(F32)
                ).astype(sbuf[a].dtype)

            along(a, line, False).start()

    def return_end(a):
        pl.when(z > 0)(lambda: along(a, z, True).wait_recv())
        pl.when(z < lines - 1)(lambda: along(a, z, False).wait_recv())
        total = base(a, z)
        total = total + jnp.where(z > 0, ubuf[a][z].astype(F32), 0.0)
        total = total + jnp.where(z < lines - 1, dbuf[a][z].astype(F32), 0.0)
        out[a][...] = total.astype(out[a].dtype)
        for line in range(lines):
            across(a, line).wait_send()
            pl.when(z != line)(lambda: along(a, line, True).wait_send())

    def nt(left, right):
        return lax.dot_general(left, right, (((1,), (1,)), ((), ())), preferred_element_type=F32)

    greet(z, y, lines, (core, over))
    begin(0)
    begin(1)
    for s in range(1, lines):
        forward(0, s)
    arrive(0)
    tables = tall[...].reshape(2 * lines, 2 * lines, tok_rows)
    chosen = lax.broadcasted_iota(jnp.int32, tables.shape, 1) == me
    weight = jnp.sum(jnp.where(chosen, tables, 0.0), axis=1)
    routed = weight > 0.0
    upto = lax.broadcasted_iota(jnp.int32, (tok_rows, tok_rows), 0) <= lax.broadcasted_iota(
        jnp.int32, (tok_rows, tok_rows), 1
    )
    count = jnp.dot(
        jnp.where(routed, 1.0, 0.0), jnp.where(upto, 1.0, 0.0), preferred_element_type=F32
    )
    forward(1, 1)
    gates = [jnp.zeros((q, 1), F32) for _ in range(4)]
    before = jnp.zeros((1, 1), F32)
    for src in range(2 * lines):
        row = slice(src, src + 1)
        rank = jnp.where(routed[row], count[row] - 1.0 + before, -1.0)
        before = before + count[row, tok_rows - 1:]
        for b in range(4):
            owner = (xc + b // 2) % 2 * 2 + (cc + b % 2) % 2
            ids = (lax.broadcasted_iota(jnp.int32, (q, tok_rows), 0) + owner * q).astype(F32)
            hit = ids == rank
            pick[b * q:(b + 1) * q, src * tok_rows:(src + 1) * tok_rows] = jnp.where(hit, 1.0, 0.0).astype(BF)
            gates[b] = gates[b] + jnp.sum(jnp.where(hit, weight[row], 0.0), axis=1, keepdims=True)
        if src == 3:
            forward(1, 2)
    for b in range(4):
        gate_out[b * q:(b + 1) * q, :] = jnp.broadcast_to(gates[b], (q, 128))
    for s in range(3, lines):
        forward(1, s)
    begin(2)
    arrive(1)
    rows_dot(xs, pick, xall, 0, 2 * q)
    forward(2, 1)
    rows_dot(part.at[0], xs, wg, 0, 2 * q)
    for i in range(2):
        to_core(0, i).start()
    forward(2, 2)
    rows_dot(part.at[1], xs, wu, 0, 2 * q)
    for i in range(2):
        to_core(1, i).start()
    send_sum(0)
    send_sum(1)
    for s in range(3, lines):
        forward(2, s)
    take_sum(0)
    take_sum(1)
    gate_pre, up_pre = fbuf[0], fbuf[1]
    hidden[:q, :] = (gate_pre * jax.nn.sigmoid(gate_pre) * up_pre).astype(BF)
    share(0)
    arrive(2)
    rows_dot(cs, pick, call, 0, 2 * q)
    rows_dot(part.at[2], cs, wd, 1, 2 * q)
    for i in range(2):
        to_core(2, i).start()
    send_sum(2)

    def finish(m):
        share_over(m).wait_recv()
        share_core(m, 1).start()

    def whole(m):
        for i in range(2):
            share_core(m, i).wait_recv()

    finish(0)
    whole(0)

    @pl.loop(0, 2)
    def _(i):
        at = pl.ds(pl.multiple_of(i * 2 * q, 2 * q), 2 * q)
        mid[at, :] = (
            jnp.dot(hidden[at, :], wd[...], preferred_element_type=F32) * gate_out[at, :1]
        ).astype(BF)
        scaled[at, :] = (hidden[at, :].astype(F32) * gate_out[at, :1]).astype(BF)

    cols_dot(out_all, pick, mid, halves(pick.shape[1]))
    return_begin(1)
    take_sum(2)

    gate_pre, up_pre, raw = fbuf[0], fbuf[1], fbuf[2]
    sig = jax.nn.sigmoid(gate_pre)
    active = gate_pre * sig
    grad = raw * gate_out[:q, :1]
    gpg[:q, :] = (grad * up_pre * sig * (1.0 + gate_pre * (1.0 - sig))).astype(BF)
    share(1)
    upg[:q, :] = (grad * active).astype(BF)
    share(2)
    inner[0] = jnp.broadcast_to(jnp.sum(active * up_pre * raw, axis=1, keepdims=True), (q, 128))
    cols_dot(wd_grad, scaled, cs, halves(scaled.shape[1]))
    return_step(1, lines - 1)
    finish(1)
    for s in range(lines - 2, 1, -1):
        return_step(1, s)
    finish(2)
    whole(1)
    whole(2)
    share(3)

    @pl.loop(0, 2)
    def _(i):
        at = pl.ds(pl.multiple_of(i * 2 * q, 2 * q), 2 * q)
        mid[at, :] = (nt(gpg[at, :], wg[...]) + nt(upg[at, :], wu[...])).astype(BF)

    cols_dot(pair_all, pick, mid, halves(pick.shape[1]))
    return_begin(2)
    return_step(1, 1)
    finish(3)
    whole(3)
    sums = jnp.zeros((1, pick.shape[1]), F32)
    for b in range(4):
        sums = sums + jnp.sum(
            pick[b * q:(b + 1) * q, :].astype(F32) * inner[b][:, :1], axis=0, keepdims=True
        )
    for dst in range(2 * lines):
        row = sums[:, dst * tok_rows:(dst + 1) * tok_rows]
        mine = lax.broadcasted_iota(jnp.int32, (2 * lines, tok_rows), 0) == me
        inner_all[dst * 2 * lines:(dst + 1) * 2 * lines, :] = jnp.where(mine, row, 0.0)
    return_begin(0)
    cols_dot(wg_grad, xs, gpg, halves(xs.shape[1]))
    for s in range(lines - 1, 0, -1):
        return_step(2, s)
        return_step(0, s)
        if s == lines - 1:
            cols_dot(wu_grad, xs, upg, halves(xs.shape[1]))
    return_end(1)
    return_end(0)
    return_end(2)
    for m in range(4):
        share_over(m).wait_send()
        for i in range(2):
            share_core(m, i).wait_send()
    for m in range(3):
        to_over(m).wait_send()
        for i in range(2):
            to_core(m, i).wait_send()
    for a in range(3):
        for line in range(lines):
            move(a, 2, line * 2 + y, partner).wait_send()

            @pl.when((line <= z) & (z < lines - 1))
            def _():
                move(a, 0, line * 2 + y, partner).wait_send()

            @pl.when((line >= z) & (z > 0))
            def _():
                move(a, 1, line * 2 + y, partner).wait_send()


def layer(experts, slots, table, tok, cot, wg, wu, wd):
    tok_rows, quarter = tok.shape
    width, q = wd.shape[0], slots // 4
    half = [pltpu.VMEM((experts // 2,) + b.shape, b.dtype) for b in (table, tok, tok)]
    sds = jax.ShapeDtypeStruct
    dma = pltpu.SemaphoreType.DMA
    blocks = pltpu.VMEM((3, q, width), BF)
    return pl.pallas_call(
        functools.partial(layer_kernel, experts // 2),
        out_shape=[sds(table.shape, F32), sds(tok.shape, BF), sds(tok.shape, BF)]
        + [sds(w.shape, BF) for w in (wg, wu, wd)],
        in_specs=[VM] * 6,
        out_specs=[VM] * 6,
        scratch_shapes=[
            pltpu.VMEM((slots, width), BF),
            pltpu.VMEM((slots, width), BF),
            pltpu.VMEM((slots, width), BF),
            pltpu.VMEM((4, q, 128), F32),
            pltpu.VMEM((slots, quarter), BF),
            pltpu.VMEM((slots, quarter), BF),
            pltpu.VMEM((slots, experts * tok_rows), BF),
            pltpu.VMEM((slots, 128), F32),
            pltpu.VMEM((experts * experts, tok_rows), F32),
            pltpu.VMEM((experts * tok_rows, quarter), BF),
            pltpu.VMEM((experts * tok_rows, quarter), BF),
            pltpu.VMEM((3, slots, width), BF),
            pltpu.VMEM((3, 2, q, width), BF),
            blocks,
            blocks,
            pltpu.VMEM((3, q, width), F32),
            pltpu.VMEM((slots, quarter), BF),
            pltpu.VMEM((slots, width), BF),
            pltpu.VMEM((experts * experts, tok_rows), F32),
            pltpu.VMEM((experts * tok_rows, quarter), BF),
            pltpu.VMEM((experts * tok_rows, quarter), BF),
        ]
        + half * 4
        + [
            dma((3, 3, experts)),
            dma((3, experts)),
            dma((3,)),
            dma((3, 2)),
            dma((3, 2)),
            dma((3,)),
            dma((3,)),
            dma((4,)),
            dma((4,)),
            dma((4, 2)),
            dma((4, 2)),
        ]
        + [dma((3, experts // 2))] * 5,
        compiler_params=pltpu.CompilerParams(
            collective_id=0, has_side_effects=True, vmem_limit_bytes=60 << 20
        ),
    )(table, tok, cot, wg, wu, wd)


def per_device(tokens, routes, gates, w_gate, w_up, w_down, cotangent):
    tok_rows, quarter = tokens.shape
    top_count = routes.shape[1]
    experts = lax.axis_size("expert")
    capacity = max(2, (3 * tok_rows * top_count + 2 * experts - 1) // (2 * experts))
    slots = experts * capacity
    q = slots // 4
    me = lax.axis_index("expert")
    d = lax.axis_index("dp")
    wg, wu, wd = w_gate[0], w_up[0], w_down[0]

    labels = jnp.arange(experts, dtype=jnp.int32)
    chosen = routes[:, :, None] == labels[None, None, :]
    table = jnp.sum(jnp.where(chosen, gates[:, :, None], 0.0), axis=1)
    near = experts == 8
    if near:
        inner, mixed, token_grad, w_gate_grad, w_up_grad, w_down_grad = layer(
            experts, slots, table.T, tokens, cotangent, wg, wu, wd
        )
        gate_grad = jnp.sum(jnp.where(chosen, inner.T[:, None, :], 0.0), axis=2)
        return mixed, token_grad, gate_grad, w_gate_grad[None], w_up_grad[None], w_down_grad[None]
    weight = lax.all_to_all(table.T, "expert", split_axis=0, concat_axis=0, tiled=True)
    x = lax.all_gather(tokens, "expert", axis=0, tiled=True)
    c = lax.all_gather(cotangent, "expert", axis=0, tiled=True)
    weight = weight.reshape(experts * tok_rows)

    routed = weight > 0.0
    rank = jnp.cumsum(routed.astype(jnp.int32)) - 1
    rank = jnp.where(routed, rank, -1)
    place = jnp.arange(slots, dtype=jnp.int32)
    place = (place // q ^ d) * q + place % q
    hit = place[:, None] == rank[None, :]
    pick = hit.astype(BF)
    slot_gate = jnp.sum(jnp.where(hit, weight[None, :], 0.0), axis=1)

    xs = dot(pick, x).astype(BF)
    gate_pre = reduce_rows(dot(xs, wg).astype(BF))
    up_pre = reduce_rows(dot(xs, wu).astype(BF))
    cs = dot(pick, c).astype(BF)
    raw_grad = reduce_rows(dot_nt(cs, wd).astype(BF))

    own_gate = slot_gate[:q, None]
    sig = jax.nn.sigmoid(gate_pre)
    active = gate_pre * sig
    hidden32 = active * up_pre
    hidden = gather_rows(hidden32.astype(BF))
    gate_inner = jnp.sum(hidden32 * raw_grad, axis=1)
    hidden_grad = raw_grad * own_gate
    gpg = gather_rows((hidden_grad * up_pre * sig * (1.0 + gate_pre * (1.0 - sig))).astype(BF))
    upg = gather_rows((hidden_grad * active).astype(BF))

    inner = gather_rows(gate_inner[:, None])

    out = (dot(hidden, wd) * slot_gate[:, None]).astype(BF)
    out = dot_t(pick, out).astype(BF)
    pair = (dot_nt(gpg, wg) + dot_nt(upg, wu)).astype(BF)
    pair = dot_t(pick, pair).astype(BF)

    inner = jnp.sum(jnp.where(pick > 0, inner, 0.0), axis=0).reshape(experts, tok_rows)
    inner = lax.all_to_all(inner, "expert", split_axis=0, concat_axis=0, tiled=True)
    mixed = lax.psum_scatter(out, "expert", scatter_dimension=0, tiled=True)
    token_grad = lax.psum_scatter(pair, "expert", scatter_dimension=0, tiled=True)
    gate_grad = jnp.sum(jnp.where(chosen, inner.T[:, None, :], 0.0), axis=2)

    w_down_grad = dot_t((hidden.astype(F32) * slot_gate[:, None]).astype(BF), cs).astype(BF)[None]
    w_gate_grad = dot_t(xs, gpg).astype(BF)[None]
    w_up_grad = dot_t(xs, upg).astype(BF)[None]
    return mixed, token_grad, gate_grad, w_gate_grad, w_up_grad, w_down_grad


def solution(mesh):
    placed = (
        P("expert", "dp"),
        P("expert", None),
        P("expert", None),
        P("expert", "dp", None),
        P("expert", "dp", None),
        P("expert", None, "dp"),
        P("expert", "dp"),
    )
    return jax.shard_map(
        per_device,
        mesh=mesh,
        in_specs=placed,
        out_specs=(
            P("expert", "dp"),
            P("expert", "dp"),
            P("expert", None),
            P("expert", "dp", None),
            P("expert", "dp", None),
            P("expert", None, "dp"),
        ),
        check_vma=False,
    )
```
